256 devices in a mesh: ctx: 64 (over z, y, core), head: 4 (over x).
Axes of the slice: x: 4, y: 4, z: 8, core: 2. Of those that a mesh axis runs over, the one named last changes fastest.
Arguments:
- queries: bfloat16 [8192, 36864], P('ctx', 'head'), may hold values from -25 to 25
- cache_latent: bfloat16 [262144, 576], P('ctx'), may hold values from -4 to 4
- cache_scales: float32 [262144, 5], P('ctx'), may hold values from 0.3 to 3
- index_keys: bfloat16 [262144, 128], P('ctx'), may hold values from -6 to 6
- index_queries: bfloat16 [8192, 8192], P('ctx', 'head'), may hold values from -6 to 6
- index_weights: bfloat16 [8192, 64], P('ctx', 'head'), may hold values from -0.75 to 0.75
- value_up: bfloat16 [64, 512, 128], P('head'), may hold values from -1 to 1
- selections: int32 [128, 32], P('ctx'), may hold values from 0 to 4095, as said below
Outputs:
- attn_out: bfloat16 [8192, 8192], P('ctx', 'head')
- index_logits: float32 [8192, 2048], P('ctx', 'head')
The draws below stay inside these ranges and needn't reach their ends.
Inputs may be any that keep to these rules, and one draw needn't show every extreme that they name: `selections`: row r names 32 different blocks by global index, block b holding cache tokens b * 64 to b * 64 + 63 and lying on ctx index b // 64. No named block lies after d(r) = (r // 2) * 64 + 62 + r % 2, the block of row r's own query tokens, and d(r) is always named. Over the 2 rows of one ctx index, the named blocks that lie on any one other ctx index are at most 2 different ones; for ctx index 0 they are exactly 2, from every other ctx index.
All inputs are finite; a program needn't handle non-finite values.
Results may differ from the reference program's by a relative error of at most 0.014.
Values may be sent and summed in bfloat16 or wider, within the bound.
A program may use at most 128 MiB of HBM per device.

```python
import math
import jax
import jax.numpy as jnp
import numpy as np
from jax import lax

HEADS = 64
D_LAT = 512
D_ROPE = 64
NOPE_DIM = 128
D_HEAD = 128
IDX_HEADS = 64
IDX_DIM = 128
BLOCK = 64
SEL = 32
D_KEY = 576
QB_DEV = 2
KB_DEV = 64
QTOKENS = 8192
CTOKENS = 262144
QBLOCKS = 128


def cache_noise(key):
    noise_key = jax.random.fold_in(key, 101)
    first_key = jax.random.fold_in(noise_key, 0)
    gauss_part = jax.random.truncated_normal(first_key, -4.0, 4.0, (CTOKENS, D_KEY), jnp.float32)
    return gauss_part


def draw_queries(key, part):
    key = jax.random.fold_in(key, 7)
    values = 0.5 * jax.random.truncated_normal(key, -6.0, 6.0, (QTOKENS, HEADS * D_KEY), jnp.float32)
    return values.astype(jnp.bfloat16)


def draw_cache_latent(key, part):
    gauss_part = cache_noise(key)
    values = gauss_part
    return values.astype(jnp.bfloat16)


def draw_cache_scales(key, part):
    key = jax.random.fold_in(key, 9)
    scales = 0.3 * jnp.exp(jax.random.uniform(key, (CTOKENS, 5), jnp.float32, 0.0, math.log(10.0)))
    return jnp.clip(scales, 0.3, 3.0)


def row_layout():
    layout = []
    start_at = QB_DEV + 2
    for row_index in range(QB_DEV):
        if row_index == 0:
            entries = [0, QB_DEV, QB_DEV + 1] + list(range(start_at, start_at + SEL - 3))
            start_at = start_at + SEL - 3
        else:
            entries = [row_index, QB_DEV] + list(range(start_at, start_at + SEL - 2))
            start_at = start_at + SEL - 2
        layout.append(entries)
    return np.array(layout, dtype=np.int32)


def device_rows(row_key, ctx_place):
    ctx_total = QBLOCKS // QB_DEV
    sub_keys = jax.random.split(row_key, 6)
    row_lead = jnp.arange(QB_DEV, dtype=jnp.int32)
    diagonals = ctx_place * KB_DEV + KB_DEV - QB_DEV + row_lead
    own_index = jnp.arange(KB_DEV, dtype=jnp.int32)
    own_score = jax.random.randint(sub_keys[0], (QB_DEV, KB_DEV), 0, 32768, jnp.int32) * 4096 + own_index[None, :]
    own_valid = own_index[None, :] < (KB_DEV - QB_DEV + row_lead)[:, None]
    own_score = jnp.where(own_valid, own_score + (1 << 28), own_score)
    own_pick = lax.top_k(own_score, SEL - 1)[1].astype(jnp.int32)
    first_rows = jnp.concatenate([diagonals[:, None], ctx_place * KB_DEV + own_pick], axis=1)
    sink_block = jax.random.randint(sub_keys[1], (1,), 1, KB_DEV, jnp.int32)
    first_pick = jax.random.randint(sub_keys[2], (ctx_total, 1), 0, KB_DEV, jnp.int32)
    second_pick = (first_pick + jax.random.randint(sub_keys[3], (ctx_total, 1), 1, KB_DEV, jnp.int32)) % KB_DEV
    owner_ids = jnp.arange(ctx_total, dtype=jnp.int32)[:, None]
    remote_ids = (owner_ids * KB_DEV + jnp.concatenate([first_pick, second_pick], axis=1)).reshape(-1)
    remote_ok = jnp.broadcast_to((owner_ids >= 1) & (owner_ids < ctx_place), (ctx_total, 2)).reshape(-1)
    pool_ids = jnp.concatenate([remote_ids, ctx_place * KB_DEV + own_index])
    pool_level = jnp.concatenate([jnp.where(remote_ok, 2, 0), jnp.where(own_index < KB_DEV - QB_DEV, 1, 0)]).astype(jnp.int32)
    pool_size = pool_ids.shape[0]
    pool_score = pool_level * (1 << 28) + jax.random.randint(sub_keys[4], (pool_size,), 0, 32768, jnp.int32) * 4096 + jnp.arange(pool_size, dtype=jnp.int32)
    pool_order = lax.top_k(pool_score, QB_DEV * (SEL - 2) - 1)[1]
    stock_ids = jnp.concatenate([diagonals, jnp.zeros((1,), jnp.int32), sink_block, pool_ids[pool_order]])
    later_rows = stock_ids[row_layout()]
    all_rows = jnp.where(ctx_place == 0, first_rows, later_rows)
    shuffle = jax.random.randint(sub_keys[5], (QB_DEV, SEL), 0, 32768, jnp.int32) * 1024 + jnp.arange(SEL, dtype=jnp.int32)[None, :]
    order_rows = jnp.argsort(shuffle, axis=1, stable=True)
    return jnp.take_along_axis(all_rows, order_rows, axis=1)


def draw_selections(key, part):
    key = jax.random.fold_in(key, 13)
    ctx_total = QBLOCKS // QB_DEV
    device_keys = jax.random.split(key, ctx_total)
    rows_all = jax.vmap(device_rows)(device_keys, jnp.arange(ctx_total, dtype=jnp.int32))
    return rows_all.reshape(QBLOCKS, SEL).astype(jnp.int32)


def steps_of(key, shape, shards, low, high):
    gain = 1.0
    for axis_at, shards_of in shards:
        heights = jax.random.uniform(jax.random.fold_in(jax.random.fold_in(key, 6), axis_at), (shards_of,), jnp.float32, low / len(shards), high / len(shards))
        gain = gain * jnp.repeat(jnp.exp(heights), shape[axis_at] // shards_of).reshape((-1,) + (1,) * (len(shape) - 1 - axis_at))
    return gain


def bell_draw(stream_key, dims, scale, limit, cuts=(), held_as=jnp.bfloat16):
    drawn = jax.random.normal(stream_key, dims, jnp.float32) * scale
    if len(cuts) > 0:
        drawn = steps_of(stream_key, dims, cuts, -0.22, 0.18) * drawn
    return jnp.clip(drawn, min=-limit, max=limit).astype(held_as)


def setup_inputs(seed: int = 0) -> dict:
    streams_of = jax.random.split(jax.random.key(seed), 9)
    return {
        "queries": draw_queries(jax.random.fold_in(streams_of[8], 71), 0),
        "cache_latent": draw_cache_latent(jax.random.fold_in(streams_of[8], 71), 0),
        "cache_scales": draw_cache_scales(jax.random.fold_in(streams_of[8], 71), 0),
        "index_keys": bell_draw(streams_of[3], (CTOKENS, IDX_DIM), 1.0, 6.0, ((0, 64),)),
        "index_queries": bell_draw(streams_of[4], (QTOKENS, IDX_HEADS * IDX_DIM), 1.0, 6.0, ((0, 64), (1, 4))),
        "index_weights": bell_draw(streams_of[5], (QTOKENS, IDX_HEADS), IDX_HEADS ** -0.5, 0.75, ((0, 64), (1, 4))),
        "value_up": bell_draw(streams_of[6], (HEADS, D_LAT, D_HEAD), (D_LAT // 16) ** -0.5, 1.0, ((0, 4),)),
        "selections": draw_selections(jax.random.fold_in(streams_of[8], 71), 0),
    }


def dequantize(cache_latent, cache_scales, index_keys):
    tok_count = cache_latent.shape[0]
    group_width = D_LAT // 4
    latent_nope = cache_latent[:, :D_LAT].astype(jnp.float32).reshape(tok_count, 4, group_width)
    latent_nope = (latent_nope * cache_scales[:, :4, None]).reshape(tok_count, D_LAT)
    latent_full = jnp.concatenate([latent_nope, cache_latent[:, D_LAT:].astype(jnp.float32)], axis=1)
    idx_key = index_keys.astype(jnp.float32) * cache_scales[:, 4:5]
    return latent_full.astype(jnp.bfloat16), idx_key.astype(jnp.bfloat16)


def visibility(chosen, diagonal):
    offsets = jnp.arange(BLOCK, dtype=jnp.int32)
    earlier = chosen < diagonal
    later_ok = offsets[None, :] <= offsets[:, None]
    visible = earlier[None, :, None] | later_ok[:, None, :]
    return visible.reshape(BLOCK, SEL * BLOCK)


def reference(queries, cache_latent, cache_scales, index_keys, index_queries, index_weights, value_up, selections):
    latent, idx_key = dequantize(cache_latent, cache_scales, index_keys)
    latent_blocks = latent.reshape(CTOKENS // BLOCK, BLOCK, D_KEY)
    key_blocks = idx_key.reshape(CTOKENS // BLOCK, BLOCK, IDX_DIM)
    block_rows = jnp.arange(QBLOCKS, dtype=jnp.int32)
    diagonals = (block_rows // QB_DEV) * KB_DEV + KB_DEV - QB_DEV + block_rows % QB_DEV
    up_proj = value_up.astype(jnp.float32)
    score_scale = (NOPE_DIM + D_ROPE) ** -0.5

    def one_block(block_items):
        query_rows, iquery, iweight, chosen, diagonal = block_items
        picked = latent_blocks[chosen].reshape(SEL * BLOCK, D_KEY).astype(jnp.float32)
        picked_keys = key_blocks[chosen].reshape(SEL * BLOCK, IDX_DIM).astype(jnp.float32)
        visible = visibility(chosen, diagonal)
        scores = jnp.einsum("bhd,kd->bhk", query_rows.astype(jnp.float32), picked) * score_scale
        masked = jnp.where(visible[:, None, :], scores, -1e30)
        top_score = jnp.max(masked, axis=2, keepdims=True)
        weights = jnp.where(visible[:, None, :], jnp.exp(masked - top_score), 0.0)
        prob_rows = (weights / jnp.sum(weights, axis=2, keepdims=True)).astype(jnp.bfloat16)
        attended = jnp.einsum("bhk,kd->bhd", prob_rows.astype(jnp.float32), picked[:, :D_LAT]).astype(jnp.bfloat16)
        head_out = jnp.einsum("bhd,hde->bhe", attended.astype(jnp.float32), up_proj).astype(jnp.bfloat16)
        idx_dots = jnp.einsum("bgd,kd->bgk", iquery.astype(jnp.float32), picked_keys) * IDX_DIM ** -0.5
        logits = jnp.sum(iweight.astype(jnp.float32)[:, :, None] * jnp.maximum(idx_dots, 0.0), axis=1)
        return head_out.reshape(BLOCK, HEADS * D_HEAD), jnp.where(visible, logits, 0.0)

    attn_rows, logit_rows = lax.map(one_block, (
        queries.reshape(QBLOCKS, BLOCK, HEADS, D_KEY),
        index_queries.reshape(QBLOCKS, BLOCK, IDX_HEADS, IDX_DIM),
        index_weights.reshape(QBLOCKS, BLOCK, IDX_HEADS),
        selections,
        diagonals))
    return attn_rows.reshape(QTOKENS, HEADS * D_HEAD), logit_rows.reshape(QTOKENS, SEL * BLOCK)
```

```python
from functools import partial

import jax
import jax.numpy as jnp
from jax import lax
from jax.experimental import pallas as pl
from jax.experimental.pallas import tpu as pltpu
from jax.sharding import PartitionSpec as P

D_LAT = 512
D_ROPE = 64
NOPE_DIM = 128
D_HEAD = 128
IDX_DIM = 128
BLOCK = 64
SEL = 32
D_KEY = 576
LANES = 128
MESH = pl.DeviceIdType.MESH
BF16 = jnp.bfloat16
F32 = jnp.float32
KEY_ROWS = IDX_DIM // 4
ROPE_ROWS = D_ROPE // 4
PARTS = (KEY_ROWS + ROPE_ROWS, 32, 32, 32, 32)
STEP = 4
APART = 8
VMEM_LIMIT = 60 * 1024 * 1024


def loop(low, high, step, unroll=None):
    def body(i, carry):
        step(i)
        return carry

    lax.fori_loop(low, high, body, 0, unroll=unroll)


def lanes_at(i):
    return pl.ds(pl.multiple_of(i * LANES, LANES), LANES)


def kernel(
    n,
    heads,
    sel_ref,
    w_ref,
    lat_hbm,
    keys_hbm,
    scales_hbm,
    q_hbm,
    iq_hbm,
    up_hbm,
    out_ref,
    logits_ref,
    latq,
    ropeq,
    keyq,
    scl,
    q,
    iq,
    up,
    reqs,
    req_in,
    req_rows,
    req_smem,
    picks_v,
    picks,
    lows,
    sends,
    recvs,
    lat,
    tail,
    key,
    wcol,
    terms,
    terms_in,
    qs,
    qr,
    load_sem,
    req_send,
    req_recv,
    send_sem,
    recv_sem,
    xsend,
    xrecv,
    isend,
    irecv,
    ready,
):
    me = lax.axis_index("ctx")
    hx = lax.axis_index("head")
    group = D_LAT // 4
    wide = SEL * BLOCK
    tiles = latq.shape[1] // LANES
    parts = range(len(PARTS))
    starts = [sum(PARTS[1:p]) for p in parts]

    loads = [
        pltpu.make_async_copy(keys_hbm, keyq, load_sem.at[0]),
        pltpu.make_async_copy(
            lat_hbm.at[pl.ds(D_LAT + hx * ROPE_ROWS, ROPE_ROWS), :], ropeq, load_sem.at[1]
        ),
        pltpu.make_async_copy(scales_hbm, scl, load_sem.at[2]),
        pltpu.make_async_copy(lat_hbm.at[pl.ds(hx * group, group), :], latq, load_sem.at[3]),
    ]
    later = [
        pltpu.make_async_copy(iq_hbm, iq, load_sem.at[4]),
        pltpu.make_async_copy(q_hbm, q, load_sem.at[5]),
        pltpu.make_async_copy(up_hbm, up, load_sem.at[6]),
    ]
    for copy in loads:
        copy.start()
    req_in[...] = jnp.zeros_like(req_in)

    barrier = pltpu.get_barrier_semaphore()

    def greet(j):
        pl.semaphore_signal(
            barrier, inc=1, device_id=(lax.rem(me + j, n), hx), device_id_type=MESH
        )

    loop(1, n, greet)
    for j in range(1, heads):
        pl.semaphore_signal(
            barrier, inc=1, device_id=(me, lax.rem(hx + j, heads)), device_id_type=MESH
        )

    chosen = jnp.concatenate([sel_ref[0:1, :], sel_ref[1:2, :]], axis=1)
    count = 2 * SEL
    kblocks = 2 * tiles
    owners = chosen // kblocks
    inside = chosen - owners * kblocks
    square = (count, count)
    across = jnp.broadcast_to(chosen, square)
    diagonal = lax.broadcasted_iota(jnp.int32, square, 0) == lax.broadcasted_iota(
        jnp.int32, square, 1
    )
    down = jnp.sum(jnp.where(diagonal, across, 0), axis=1, keepdims=True)
    smaller = (down // kblocks == across // kblocks) & (down < across)
    rank = jnp.max(smaller.astype(jnp.int32), axis=0, keepdims=True)
    odd = lax.broadcasted_iota(jnp.int32, (1, count), 1) % 2
    here = (owners == me).astype(jnp.int32)
    picks_v[...] = jnp.zeros_like(picks_v)
    picks_v[0:1, 0:count] = jnp.where(here > 0, 0, owners)
    picks_v[1:2, 0:count] = jnp.where(here > 0, inside + odd - 2 * odd * (inside % 2), 0)
    picks_v[2:3, 0:count] = here
    picks_v[3:4, 0:count] = (rank != odd).astype(jnp.int32)
    for k in range(n // 8):
        owner = lax.broadcasted_iota(jnp.int32, (8, count), 0) + 8 * k
        mine = jnp.broadcast_to(owners, (8, count)) == owner
        blocks = jnp.broadcast_to(inside, (8, count))
        one = jnp.min(jnp.where(mine, blocks, kblocks - 1), axis=1, keepdims=True)
        two = jnp.max(jnp.where(mine, blocks, 0), axis=1, keepdims=True)
        two = two + 1 - 2 * (two % 2)
        lane = lax.broadcasted_iota(jnp.int32, (8, LANES), 1)
        reqs[k] = jnp.where(lane == 0, one, two)
    picks_copy = pltpu.make_async_copy(picks_v, picks, load_sem.at[7])
    picks_copy.start()

    rows_at = lax.broadcasted_iota(jnp.int32, (KEY_ROWS, IDX_DIM), 0) + hx * KEY_ROWS
    cols_at = lax.broadcasted_iota(jnp.int32, (KEY_ROWS, IDX_DIM), 1)
    take = (rows_at == cols_at).astype(BF16)
    group_at = lax.broadcasted_iota(jnp.int32, (4, LANES), 0)

    def keep(p, t, block):
        lows[p][2 * t] = block.astype(BF16)
        lows[p][2 * t + 1] = pltpu.roll(block, BLOCK, 1).astype(BF16)

    def dequantize_first(t):
        at = lanes_at(t)
        part = lax.dot_general(
            take, keyq[at, :], (((1,), (1,)), ((), ())), preferred_element_type=F32
        )
        part = part * scl[4:5, at]
        keep(0, t, jnp.concatenate([part, ropeq[:, at].astype(F32)], axis=0))

    def dequantize_rest(t):
        at = lanes_at(t)
        mine = jnp.sum(jnp.where(group_at == hx, scl[0:4, at], 0.0), axis=0, keepdims=True)
        part = latq[:, at].astype(F32) * mine
        for p in parts[1:]:
            keep(p, t, part[starts[p] : starts[p] + PARTS[p]])

    for copy in loads[:3]:
        copy.wait()
    loop(0, tiles, dequantize_first, 4)

    pl.semaphore_wait(barrier, n + heads - 2)

    def request(o, c):
        return pltpu.make_async_remote_copy(
            src_ref=reqs.at[o // 8],
            dst_ref=req_in.at[c],
            send_sem=req_send.at[o],
            recv_sem=req_recv.at[c],
            device_id=(o, hx),
            device_id_type=MESH,
        )

    loop(0, me, lambda o: request(o, me).start())

    loads[3].wait()
    loop(0, tiles, dequantize_rest, 4)
    loop(me + 1, n, lambda c: request(me, c).wait_recv())
    row_at = lax.broadcasted_iota(jnp.int32, (n, 8, LANES), 1)
    req_rows[...] = jnp.sum(jnp.where(row_at == lax.rem(me, 8), req_in[...], 0), axis=1)
    to_smem = pltpu.make_async_copy(req_rows, req_smem, load_sem.at[8])
    to_smem.start()
    to_smem.wait()

    def block_copy(p, c, o):
        return pltpu.make_async_remote_copy(
            src_ref=sends[p].at[c],
            dst_ref=recvs[p].at[o],
            send_sem=send_sem.at[p, c],
            recv_sem=recv_sem.at[p, o],
            device_id=(c, hx),
            device_id_type=MESH,
        )

    def pack(p, c):
        one = req_smem[c, 0]
        two = req_smem[c, 1]
        sends[p][c, :, 0:BLOCK] = lows[p][one][:, 0:BLOCK]
        sends[p][c, :, BLOCK:LANES] = lows[p][two][:, BLOCK:LANES]

    def pack_first(c):
        pack(0, c)
        block_copy(0, c, me).start()

    loop(me + 1, n, pack_first)
    for copy in later:
        copy.start()
    picks_copy.wait()

    def send(p):
        def step(c):
            pack(p, c)
            block_copy(p, c, me).start()

        if p > 1:
            watched = (n - 1 - me) // APART

            @pl.when(watched > 0)
            def _():
                pl.semaphore_wait(ready.at[p - 2], watched)

            loop(me + 1, n, lambda c: block_copy(p - 2, c, me).wait_send())
        loop(me + 1, n, step)

    def outs(p):
        if p == 0:
            return (
                (key, KEY_ROWS, 0, lambda part: part * KEY_ROWS),
                (tail, ROPE_ROWS, KEY_ROWS, lambda part: part * ROPE_ROWS),
            )
        return ((lat, PARTS[p], 0, lambda part: part * group + starts[p]),)

    right, left, across_x = lax.rem(hx + 1, heads), lax.rem(hx + 3, heads), lax.rem(hx + 2, heads)
    to_right, to_left, on_right, on_left = range(4)

    def share(p, i, out, way, part, peer):
        ref, rows, _, place = out
        at = pl.ds(pl.multiple_of(place(part), ROPE_ROWS), rows)
        piece = ref.at[way - 2, at, :] if way >= 2 else ref.at[:, at, :]
        return pltpu.make_async_remote_copy(
            src_ref=piece,
            dst_ref=piece,
            send_sem=xsend.at[p + len(PARTS) * i, way],
            recv_sem=xrecv.at[p + len(PARTS) * i, way],
            device_id=(me, peer),
            device_id_type=MESH,
        )

    peers = [right, left, across_x]

    def receive(p):
        loop(0, me, lambda o: block_copy(p, o, o).wait_recv())
        if p < len(PARTS) - 2:
            loop(
                1,
                me // APART + 1,
                lambda k: pl.semaphore_signal(
                    ready.at[p], inc=1, device_id=(me - APART * k, hx), device_id_type=MESH
                ),
            )
        low_lanes = lax.broadcasted_iota(jnp.int32, (PARTS[p], LANES), 1) < BLOCK

        def choose(m):
            def entry(e):
                far = recvs[p][picks[0, e]].astype(F32)
                far = jnp.where(picks[3, e] > 0, pltpu.roll(far, BLOCK, 1), far)
                near = lows[p][picks[1, e]].astype(F32)
                return jnp.where(picks[2, e] > 0, near, far)

            tile = jnp.where(low_lanes, entry(2 * m), entry(2 * m + 1)).astype(BF16)
            row = m // (SEL // 2)
            for ref, rows, first, place in outs(p):
                at = pl.ds(pl.multiple_of(place(hx), ROPE_ROWS), rows)
                ref[row, at, lanes_at(lax.rem(m, SEL // 2))] = tile[first : first + rows]

        loop(0, SEL, choose, 4)
        for i, out in enumerate(outs(p)):
            share(p, i, out, to_right, hx, right).start()
            share(p, i, out, to_left, hx, left).start()

    def forward(p):
        for i, out in enumerate(outs(p)):
            share(p, i, out, to_right, left, hx).wait_recv()
            share(p, i, out, on_right, left, right).start()
            share(p, i, out, to_left, right, hx).wait_recv()
            share(p, i, out, on_left, right, left).start()

    def shared(p):
        for i, out in enumerate(outs(p)):
            share(p, i, out, on_right, across_x, hx).wait_recv()
            share(p, i, out, on_left, across_x, hx).wait_recv()

    send(1)

    column = lax.broadcasted_iota(jnp.int32, (BLOCK, wide), 1)
    token = lax.broadcasted_iota(jnp.int32, (BLOCK, wide), 0)
    for r in range(2):
        own = me * kblocks + kblocks - 2 + r
        at = lax.broadcasted_iota(jnp.int32, (1, SEL), 1)
        place = jnp.sum(jnp.where(sel_ref[r : r + 1, :] == own, at, 0), axis=1, keepdims=True)
        hidden = (column // BLOCK == place) & (column % BLOCK > token)
        tail[r, D_ROPE:, :] = jnp.where(hidden, -1e30, 0.0).astype(BF16)
    wcol[...] = jnp.transpose(w_ref[...].astype(F32)) * IDX_DIM**-0.5

    receive(0)
    send(2)
    receive(1)
    forward(0)
    send(3)
    receive(2)
    forward(1)
    send(4)
    shared(0)

    later[0].wait()
    idx_here = wcol.shape[1]

    def index_rows(r):
        rows = pl.ds(pl.multiple_of(r * BLOCK, BLOCK), BLOCK)
        weights = wcol[rows, :]
        total = jnp.zeros((BLOCK, wide), F32)
        for g in range(idx_here):
            dots = jnp.dot(
                iq[rows, g * IDX_DIM : (g + 1) * IDX_DIM], key[r], preferred_element_type=F32
            )
            total += weights[:, g : g + 1] * jnp.maximum(dots, 0.0)
        total = jnp.where(tail[r, D_ROPE:, :].astype(F32) < 0.0, 0.0, total).astype(BF16)
        share_wide = wide // heads
        for h in range(heads):
            terms[h, rows, :] = total[:, h * share_wide : (h + 1) * share_wide]

    loop(0, 2, index_rows)

    def term(part, peer):
        return pltpu.make_async_remote_copy(
            src_ref=terms.at[peer],
            dst_ref=terms_in.at[part],
            send_sem=isend.at[peer],
            recv_sem=irecv.at[part],
            device_id=(me, peer),
            device_id_type=MESH,
        )

    for peer in peers:
        term(hx, peer).start()

    later[1].wait()
    same = (
        lax.broadcasted_iota(jnp.int32, (BLOCK, BLOCK), 0)
        == lax.broadcasted_iota(jnp.int32, (BLOCK, BLOCK), 1)
    ).astype(BF16)
    groups = up.shape[0] // STEP

    def arrange(i):
        r, g = i // groups, lax.rem(i, groups)
        part = q[
            pl.ds(pl.multiple_of(r * BLOCK, BLOCK), BLOCK),
            pl.ds(pl.multiple_of(g * STEP * D_KEY, LANES), STEP * D_KEY),
        ]
        for h in range(STEP):
            rows = slice(h * BLOCK, (h + 1) * BLOCK)
            qs[i, rows, :] = part[:, h * D_KEY : h * D_KEY + D_LAT]
            qr[i, rows, :D_ROPE] = part[:, h * D_KEY + D_LAT : (h + 1) * D_KEY]
            qr[i, rows, D_ROPE:] = same

    loop(0, 2 * groups, arrange)
    receive(3)
    forward(2)
    for peer in peers:
        term(peer, hx).wait_recv()
    logits = terms[hx].astype(F32)
    for peer in peers:
        logits += terms_in[peer].astype(F32)
    logits_ref[...] = logits

    receive(4)
    forward(3)
    forward(4)
    for p in parts[3:]:
        loop(me + 1, n, lambda c, p=p: block_copy(p, c, me).wait_send())

    later[2].wait()
    for p in parts[1:]:
        shared(p)

    def attend(i):
        r, g = i // groups, lax.rem(i, groups)
        scores = jnp.dot(qs[i], lat[r], preferred_element_type=F32)
        scores += jnp.dot(qr[i], tail[r], preferred_element_type=F32)
        top = jnp.max(scores, axis=1, keepdims=True)
        scale = (NOPE_DIM + D_ROPE) ** -0.5 * 1.4426950408889634
        weights = jnp.exp2((scores - top) * scale)
        total = jnp.sum(weights, axis=1, keepdims=True)
        attended = lax.dot_general(
            weights.astype(BF16), lat[r], (((1,), (1,)), ((), ())), preferred_element_type=F32
        )
        attended = (attended / total).astype(BF16)
        rows = pl.ds(pl.multiple_of(r * BLOCK, BLOCK), BLOCK)
        for h in range(STEP):
            out = jnp.dot(
                attended[h * BLOCK : (h + 1) * BLOCK], up[g * STEP + h], preferred_element_type=F32
            )
            out_ref[rows, lanes_at(g * STEP + h)] = out.astype(BF16)

    loop(0, 2 * groups, attend)

    for p in parts:
        for i, out in enumerate(outs(p)):
            share(p, i, out, to_right, hx, right).wait_send()
            share(p, i, out, to_left, hx, left).wait_send()
            share(p, i, out, on_right, left, right).wait_send()
            share(p, i, out, on_left, right, left).wait_send()
    for peer in peers:
        term(hx, peer).wait_send()
    loop(0, me, lambda o: request(o, me).wait_send())


def local(
    queries,
    cache_latent,
    cache_scales,
    index_keys,
    index_queries,
    index_weights,
    value_up,
    selections,
):
    n = lax.axis_size("ctx")
    heads = lax.axis_size("head")
    tokens = index_keys.shape[0]
    qtokens = queries.shape[0]
    kblocks = tokens // BLOCK
    heads_here = value_up.shape[0]
    idx_here = index_weights.shape[1]
    wide = SEL * BLOCK
    any_spec = pl.BlockSpec(memory_space=pl.ANY)
    vmem_spec = pl.BlockSpec(memory_space=pltpu.VMEM)
    dma = pltpu.SemaphoreType.DMA
    vmem = pltpu.VMEM
    steps = 2 * heads_here // STEP
    return pl.pallas_call(
        partial(kernel, n, heads),
        out_shape=(
            jax.ShapeDtypeStruct((qtokens, heads_here * D_HEAD), BF16),
            jax.ShapeDtypeStruct((qtokens, wide // heads), F32),
        ),
        in_specs=[vmem_spec] * 2 + [any_spec] * 6,
        out_specs=(vmem_spec,) * 2,
        scratch_shapes=[
            vmem((D_LAT // 4, tokens), BF16),
            vmem((ROPE_ROWS, tokens), BF16),
            vmem((tokens, IDX_DIM), BF16),
            vmem((5, tokens), F32),
            vmem(queries.shape, BF16),
            vmem(index_queries.shape, BF16),
            vmem(value_up.shape, BF16),
            vmem((n // 8, 8, LANES), jnp.int32),
            vmem((n, 8, LANES), jnp.int32),
            vmem((n, LANES), jnp.int32),
            pltpu.SMEM((n, LANES), jnp.int32),
            vmem((8, LANES), jnp.int32),
            pltpu.SMEM((8, LANES), jnp.int32),
            [vmem((kblocks, rows, LANES), BF16) for rows in PARTS],
            [vmem((n, rows, LANES), BF16) for rows in PARTS],
            [vmem((n, rows, LANES), BF16) for rows in PARTS],
            vmem((2, D_LAT, wide), BF16),
            vmem((2, D_ROPE + BLOCK, wide), BF16),
            vmem((2, IDX_DIM, wide), BF16),
            vmem((qtokens, idx_here), F32),
            vmem((heads, qtokens, wide // heads), BF16),
            vmem((heads, qtokens, wide // heads), BF16),
            vmem((steps, STEP * BLOCK, D_LAT), BF16),
            vmem((steps, STEP * BLOCK, 2 * D_ROPE), BF16),
            dma((9,)),
            dma((n,)),
            dma((n,)),
            dma((len(PARTS), n)),
            dma((len(PARTS), n)),
            dma((len(PARTS) + 1, heads)),
            dma((len(PARTS) + 1, heads)),
            dma((heads,)),
            dma((heads,)),
            pltpu.SemaphoreType.REGULAR((len(PARTS),)),
        ],
        compiler_params=pltpu.CompilerParams(
            collective_id=0, has_side_effects=True, vmem_limit_bytes=VMEM_LIMIT
        ),
        name="sparse_attention",
    )(
        selections,
        index_weights.T,
        cache_latent.T,
        index_keys,
        cache_scales.T,
        queries,
        index_queries,
        value_up,
    )


def solution(mesh):
    return jax.shard_map(
        local,
        mesh=mesh,
        in_specs=(
            P("ctx", "head"),
            P("ctx", None),
            P("ctx", None),
            P("ctx", None),
            P("ctx", "head"),
            P("ctx", "head"),
            P("head", None, None),
            P("ctx", None),
        ),
        out_specs=(P("ctx", "head"), P("ctx", "head")),
        check_vma=False,
    )
```

```python
from functools import partial

import jax
import jax.numpy as jnp
from jax import lax
from jax.experimental import pallas as pl
from jax.experimental.pallas import tpu as pltpu
from jax.sharding import PartitionSpec as P

D_LAT = 512
D_ROPE = 64
NOPE_DIM = 128
D_HEAD = 128
IDX_DIM = 128
BLOCK = 64
SEL = 32
D_KEY = 576
LANES = 128
MESH = pl.DeviceIdType.MESH
BF16 = jnp.bfloat16
F32 = jnp.float32
KEY_ROWS = IDX_DIM // 4
ROPE_ROWS = D_ROPE // 4
PARTS = (KEY_ROWS + ROPE_ROWS, 32, 32, 32, 32)
STEP = 8
APART = 8
VMEM_LIMIT = 60 * 1024 * 1024


def loop(low, high, step, unroll=None):
    def body(i, carry):
        step(i)
        return carry

    lax.fori_loop(low, high, body, 0, unroll=unroll)


def lanes_at(i):
    return pl.ds(pl.multiple_of(i * LANES, LANES), LANES)


def kernel(
    n,
    heads,
    sel_ref,
    w_ref,
    lat_hbm,
    keys_hbm,
    scales_hbm,
    q_hbm,
    iq_hbm,
    up_hbm,
    out_ref,
    logits_ref,
    latq,
    ropeq,
    keyq,
    scl,
    q,
    iq,
    up,
    reqs,
    req_in,
    req_rows,
    req_smem,
    picks_v,
    picks,
    lows,
    sends,
    recvs,
    lat,
    tail,
    key,
    wcol,
    terms,
    terms_in,
    qs,
    qr,
    load_sem,
    req_send,
    req_recv,
    send_sem,
    recv_sem,
    xsend,
    xrecv,
    isend,
    irecv,
    ready,
):
    me = lax.axis_index("ctx")
    hx = lax.axis_index("head")
    group = D_LAT // 4
    wide = SEL * BLOCK
    tiles = latq.shape[1] // LANES
    parts = range(len(PARTS))
    starts = [sum(PARTS[1:p]) for p in parts]

    loads = [
        pltpu.make_async_copy(keys_hbm, keyq, load_sem.at[0]),
        pltpu.make_async_copy(
            lat_hbm.at[pl.ds(D_LAT + hx * ROPE_ROWS, ROPE_ROWS), :], ropeq, load_sem.at[1]
        ),
        pltpu.make_async_copy(scales_hbm, scl, load_sem.at[2]),
        pltpu.make_async_copy(lat_hbm.at[pl.ds(hx * group, group), :], latq, load_sem.at[3]),
    ]
    later = [
        pltpu.make_async_copy(iq_hbm, iq, load_sem.at[4]),
        pltpu.make_async_copy(q_hbm, q, load_sem.at[5]),
        pltpu.make_async_copy(up_hbm, up, load_sem.at[6]),
    ]
    for copy in loads:
        copy.start()
    req_in[...] = jnp.zeros_like(req_in)

    barrier = pltpu.get_barrier_semaphore()

    def greet(j):
        pl.semaphore_signal(
            barrier, inc=1, device_id=(lax.rem(me + j, n), hx), device_id_type=MESH
        )

    loop(1, n, greet)
    for j in range(1, heads):
        pl.semaphore_signal(
            barrier, inc=1, device_id=(me, lax.rem(hx + j, heads)), device_id_type=MESH
        )

    chosen = jnp.concatenate([sel_ref[0:1, :], sel_ref[1:2, :]], axis=1)
    count = 2 * SEL
    kblocks = 2 * tiles
    owners = chosen // kblocks
    inside = chosen - owners * kblocks
    square = (count, count)
    across = jnp.broadcast_to(chosen, square)
    diagonal = lax.broadcasted_iota(jnp.int32, square, 0) == lax.broadcasted_iota(
        jnp.int32, square, 1
    )
    down = jnp.sum(jnp.where(diagonal, across, 0), axis=1, keepdims=True)
    smaller = (down // kblocks == across // kblocks) & (down < across)
    rank = jnp.max(smaller.astype(jnp.int32), axis=0, keepdims=True)
    odd = lax.broadcasted_iota(jnp.int32, (1, count), 1) % 2
    here = (owners == me).astype(jnp.int32)
    picks_v[...] = jnp.zeros_like(picks_v)
    picks_v[0:1, 0:count] = jnp.where(here > 0, 0, owners)
    picks_v[1:2, 0:count] = jnp.where(here > 0, inside + odd - 2 * odd * (inside % 2), 0)
    picks_v[2:3, 0:count] = here
    picks_v[3:4, 0:count] = (rank != odd).astype(jnp.int32)
    for k in range(n // 8):
        owner = lax.broadcasted_iota(jnp.int32, (8, count), 0) + 8 * k
        mine = jnp.broadcast_to(owners, (8, count)) == owner
        blocks = jnp.broadcast_to(inside, (8, count))
        one = jnp.min(jnp.where(mine, blocks, kblocks - 1), axis=1, keepdims=True)
        two = jnp.max(jnp.where(mine, blocks, 0), axis=1, keepdims=True)
        two = two + 1 - 2 * (two % 2)
        lane = lax.broadcasted_iota(jnp.int32, (8, LANES), 1)
        reqs[k] = jnp.where(lane == 0, one, two)
    picks_copy = pltpu.make_async_copy(picks_v, picks, load_sem.at[7])
    picks_copy.start()

    rows_at = lax.broadcasted_iota(jnp.int32, (KEY_ROWS, IDX_DIM), 0) + hx * KEY_ROWS
    cols_at = lax.broadcasted_iota(jnp.int32, (KEY_ROWS, IDX_DIM), 1)
    take = (rows_at == cols_at).astype(BF16)
    group_at = lax.broadcasted_iota(jnp.int32, (4, LANES), 0)

    def keep(p, t, block):
        lows[p][2 * t] = block.astype(BF16)
        lows[p][2 * t + 1] = pltpu.roll(block, BLOCK, 1).astype(BF16)

    def dequantize_first(t):
        at = lanes_at(t)
        part = lax.dot_general(
            take, keyq[at, :], (((1,), (1,)), ((), ())), preferred_element_type=F32
        )
        part = part * scl[4:5, at]
        keep(0, t, jnp.concatenate([part, ropeq[:, at].astype(F32)], axis=0))

    def dequantize_rest(t):
        at = lanes_at(t)
        mine = jnp.sum(jnp.where(group_at == hx, scl[0:4, at], 0.0), axis=0, keepdims=True)
        part = latq[:, at].astype(F32) * mine
        for p in parts[1:]:
            keep(p, t, part[starts[p] : starts[p] + PARTS[p]])

    for copy in loads[:3]:
        copy.wait()
    loop(0, tiles, dequantize_first, 4)

    pl.semaphore_wait(barrier, n + heads - 2)

    def request(o, c):
        return pltpu.make_async_remote_copy(
            src_ref=reqs.at[o // 8],
            dst_ref=req_in.at[c],
            send_sem=req_send.at[o],
            recv_sem=req_recv.at[c],
            device_id=(o, hx),
            device_id_type=MESH,
        )

    loop(0, me, lambda o: request(o, me).start())

    loads[3].wait()
    loop(0, tiles, dequantize_rest, 4)
    loop(me + 1, n, lambda c: request(me, c).wait_recv())
    row_at = lax.broadcasted_iota(jnp.int32, (n, 8, LANES), 1)
    req_rows[...] = jnp.sum(jnp.where(row_at == lax.rem(me, 8), req_in[...], 0), axis=1)
    to_smem = pltpu.make_async_copy(req_rows, req_smem, load_sem.at[8])
    to_smem.start()
    to_smem.wait()

    def block_copy(p, c, o):
        return pltpu.make_async_remote_copy(
            src_ref=sends[p].at[c],
            dst_ref=recvs[p].at[o],
            send_sem=send_sem.at[p, c],
            recv_sem=recv_sem.at[p, o],
            device_id=(c, hx),
            device_id_type=MESH,
        )

    def pack(p, c):
        one = req_smem[c, 0]
        two = req_smem[c, 1]
        sends[p][c, :, 0:BLOCK] = lows[p][one][:, 0:BLOCK]
        sends[p][c, :, BLOCK:LANES] = lows[p][two][:, BLOCK:LANES]

    def pack_first(c):
        pack(0, c)
        block_copy(0, c, me).start()

    loop(me + 1, n, pack_first)
    for copy in later:
        copy.start()
    picks_copy.wait()

    def send(p):
        def step(c):
            pack(p, c)
            block_copy(p, c, me).start()

        if p > 1:
            watched = (n - 1 - me) // APART

            @pl.when(watched > 0)
            def _():
                pl.semaphore_wait(ready.at[p - 2], watched)

            loop(me + 1, n, lambda c: block_copy(p - 2, c, me).wait_send())
        loop(me + 1, n, step)

    def outs(p):
        if p == 0:
            return (
                (key, KEY_ROWS, 0, lambda part: part * KEY_ROWS),
                (tail, ROPE_ROWS, KEY_ROWS, lambda part: part * ROPE_ROWS),
            )
        return ((lat, PARTS[p], 0, lambda part: part * group + starts[p]),)

    right, left, across_x = lax.rem(hx + 1, heads), lax.rem(hx + 3, heads), lax.rem(hx + 2, heads)
    to_right, to_left, on_right, on_left = range(4)

    def share(p, i, out, way, part, peer):
        ref, rows, _, place = out
        at = pl.ds(pl.multiple_of(place(part), ROPE_ROWS), rows)
        piece = ref.at[way - 2, at, :] if way >= 2 else ref.at[:, at, :]
        return pltpu.make_async_remote_copy(
            src_ref=piece,
            dst_ref=piece,
            send_sem=xsend.at[p + len(PARTS) * i, way],
            recv_sem=xrecv.at[p + len(PARTS) * i, way],
            device_id=(me, peer),
            device_id_type=MESH,
        )

    peers = [right, left, across_x]

    def receive(p):
        loop(0, me, lambda o: block_copy(p, o, o).wait_recv())
        if p < len(PARTS) - 2:
            loop(
                1,
                me // APART + 1,
                lambda k: pl.semaphore_signal(
                    ready.at[p], inc=1, device_id=(me - APART * k, hx), device_id_type=MESH
                ),
            )
        low_lanes = lax.broadcasted_iota(jnp.int32, (PARTS[p], LANES), 1) < BLOCK

        def choose(m):
            def entry(e):
                far = recvs[p][picks[0, e]].astype(F32)
                far = jnp.where(picks[3, e] > 0, pltpu.roll(far, BLOCK, 1), far)
                near = lows[p][picks[1, e]].astype(F32)
                return jnp.where(picks[2, e] > 0, near, far)

            tile = jnp.where(low_lanes, entry(2 * m), entry(2 * m + 1)).astype(BF16)
            row = m // (SEL // 2)
            for ref, rows, first, place in outs(p):
                at = pl.ds(pl.multiple_of(place(hx), ROPE_ROWS), rows)
                ref[row, at, lanes_at(lax.rem(m, SEL // 2))] = tile[first : first + rows]

        loop(0, SEL, choose, 4)
        for i, out in enumerate(outs(p)):
            share(p, i, out, to_right, hx, right).start()
            share(p, i, out, to_left, hx, left).start()

    def forward(p):
        for i, out in enumerate(outs(p)):
            share(p, i, out, to_right, left, hx).wait_recv()
            share(p, i, out, on_right, left, right).start()
            share(p, i, out, to_left, right, hx).wait_recv()
            share(p, i, out, on_left, right, left).start()

    def shared(p):
        for i, out in enumerate(outs(p)):
            share(p, i, out, on_right, across_x, hx).wait_recv()
            share(p, i, out, on_left, across_x, hx).wait_recv()

    send(1)

    column = lax.broadcasted_iota(jnp.int32, (BLOCK, wide), 1)
    token = lax.broadcasted_iota(jnp.int32, (BLOCK, wide), 0)
    for r in range(2):
        own = me * kblocks + kblocks - 2 + r
        at = lax.broadcasted_iota(jnp.int32, (1, SEL), 1)
        place = jnp.sum(jnp.where(sel_ref[r : r + 1, :] == own, at, 0), axis=1, keepdims=True)
        hidden = (column // BLOCK == place) & (column % BLOCK > token)
        tail[r, D_ROPE:, :] = jnp.where(hidden, -1e30, 0.0).astype(BF16)
    wcol[...] = jnp.transpose(w_ref[...].astype(F32)) * IDX_DIM**-0.5

    receive(0)
    send(2)
    receive(1)
    forward(0)
    send(3)
    receive(2)
    forward(1)
    send(4)
    shared(0)

    later[0].wait()
    idx_here = wcol.shape[1]

    def index_rows(r):
        rows = pl.ds(pl.multiple_of(r * BLOCK, BLOCK), BLOCK)
        weights = wcol[rows, :]
        total = jnp.zeros((BLOCK, wide), F32)
        for g in range(idx_here):
            dots = jnp.dot(
                iq[rows, g * IDX_DIM : (g + 1) * IDX_DIM], key[r], preferred_element_type=F32
            )
            total += weights[:, g : g + 1] * jnp.maximum(dots, 0.0)
        total = jnp.where(tail[r, D_ROPE:, :].astype(F32) < 0.0, 0.0, total).astype(BF16)
        share_wide = wide // heads
        for h in range(heads):
            terms[h, rows, :] = total[:, h * share_wide : (h + 1) * share_wide]

    loop(0, 2, index_rows)

    def term(part, peer):
        return pltpu.make_async_remote_copy(
            src_ref=terms.at[peer],
            dst_ref=terms_in.at[part],
            send_sem=isend.at[peer],
            recv_sem=irecv.at[part],
            device_id=(me, peer),
            device_id_type=MESH,
        )

    for peer in peers:
        term(hx, peer).start()

    later[1].wait()
    same = (
        lax.broadcasted_iota(jnp.int32, (BLOCK, BLOCK), 0)
        == lax.broadcasted_iota(jnp.int32, (BLOCK, BLOCK), 1)
    ).astype(BF16)
    groups = up.shape[0] // STEP

    def arrange(i):
        r, g = i // groups, lax.rem(i, groups)
        part = q[
            pl.ds(pl.multiple_of(r * BLOCK, BLOCK), BLOCK),
            pl.ds(pl.multiple_of(g * STEP * D_KEY, LANES), STEP * D_KEY),
        ]
        for h in range(STEP):
            rows = slice(h * BLOCK, (h + 1) * BLOCK)
            qs[i, rows, :] = part[:, h * D_KEY : h * D_KEY + D_LAT]
            qr[i, rows, :D_ROPE] = part[:, h * D_KEY + D_LAT : (h + 1) * D_KEY]
            qr[i, rows, D_ROPE:] = same

    loop(0, 2 * groups, arrange)
    receive(3)
    forward(2)
    for peer in peers:
        term(peer, hx).wait_recv()
    logits = terms[hx].astype(F32)
    for peer in peers:
        logits += terms_in[peer].astype(F32)
    logits_ref[...] = logits

    receive(4)
    forward(3)
    forward(4)
    for p in parts[3:]:
        loop(me + 1, n, lambda c, p=p: block_copy(p, c, me).wait_send())

    later[2].wait()
    for p in parts[1:]:
        shared(p)

    def attend(i):
        r, g = i // groups, lax.rem(i, groups)
        scores = jnp.dot(qs[i], lat[r], preferred_element_type=F32)
        scores += jnp.dot(qr[i], tail[r], preferred_element_type=F32)
        top = jnp.max(scores, axis=1, keepdims=True)
        scale = (NOPE_DIM + D_ROPE) ** -0.5 * 1.4426950408889634
        weights = jnp.exp2((scores - top) * scale)
        total = jnp.sum(weights, axis=1, keepdims=True)
        attended = lax.dot_general(
            weights.astype(BF16), lat[r], (((1,), (1,)), ((), ())), preferred_element_type=F32
        )
        attended = (attended / total).astype(BF16)
        rows = pl.ds(pl.multiple_of(r * BLOCK, BLOCK), BLOCK)
        for h in range(STEP):
            out = jnp.dot(
                attended[h * BLOCK : (h + 1) * BLOCK], up[g * STEP + h], preferred_element_type=F32
            )
            out_ref[rows, lanes_at(g * STEP + h)] = out.astype(BF16)

    loop(0, 2 * groups, attend)

    for p in parts:
        for i, out in enumerate(outs(p)):
            share(p, i, out, to_right, hx, right).wait_send()
            share(p, i, out, to_left, hx, left).wait_send()
            share(p, i, out, on_right, left, right).wait_send()
            share(p, i, out, on_left, right, left).wait_send()
    for peer in peers:
        term(hx, peer).wait_send()
    loop(0, me, lambda o: request(o, me).wait_send())


def local(
    queries,
    cache_latent,
    cache_scales,
    index_keys,
    index_queries,
    index_weights,
    value_up,
    selections,
):
    n = lax.axis_size("ctx")
    heads = lax.axis_size("head")
    tokens = index_keys.shape[0]
    qtokens = queries.shape[0]
    kblocks = tokens // BLOCK
    heads_here = value_up.shape[0]
    idx_here = index_weights.shape[1]
    wide = SEL * BLOCK
    any_spec = pl.BlockSpec(memory_space=pl.ANY)
    vmem_spec = pl.BlockSpec(memory_space=pltpu.VMEM)
    dma = pltpu.SemaphoreType.DMA
    vmem = pltpu.VMEM
    steps = 2 * heads_here // STEP
    return pl.pallas_call(
        partial(kernel, n, heads),
        out_shape=(
            jax.ShapeDtypeStruct((qtokens, heads_here * D_HEAD), BF16),
            jax.ShapeDtypeStruct((qtokens, wide // heads), F32),
        ),
        in_specs=[vmem_spec] * 2 + [any_spec] * 6,
        out_specs=(vmem_spec,) * 2,
        scratch_shapes=[
            vmem((D_LAT // 4, tokens), BF16),
            vmem((ROPE_ROWS, tokens), BF16),
            vmem((tokens, IDX_DIM), BF16),
            vmem((5, tokens), F32),
            vmem(queries.shape, BF16),
            vmem(index_queries.shape, BF16),
            vmem(value_up.shape, BF16),
            vmem((n // 8, 8, LANES), jnp.int32),
            vmem((n, 8, LANES), jnp.int32),
            vmem((n, LANES), jnp.int32),
            pltpu.SMEM((n, LANES), jnp.int32),
            vmem((8, LANES), jnp.int32),
            pltpu.SMEM((8, LANES), jnp.int32),
            [vmem((kblocks, rows, LANES), BF16) for rows in PARTS],
            [vmem((n, rows, LANES), BF16) for rows in PARTS],
            [vmem((n, rows, LANES), BF16) for rows in PARTS],
            vmem((2, D_LAT, wide), BF16),
            vmem((2, D_ROPE + BLOCK, wide), BF16),
            vmem((2, IDX_DIM, wide), BF16),
            vmem((qtokens, idx_here), F32),
            vmem((heads, qtokens, wide // heads), BF16),
            vmem((heads, qtokens, wide // heads), BF16),
            vmem((steps, STEP * BLOCK, D_LAT), BF16),
            vmem((steps, STEP * BLOCK, 2 * D_ROPE), BF16),
            dma((9,)),
            dma((n,)),
            dma((n,)),
            dma((len(PARTS), n)),
            dma((len(PARTS), n)),
            dma((len(PARTS) + 1, heads)),
            dma((len(PARTS) + 1, heads)),
            dma((heads,)),
            dma((heads,)),
            pltpu.SemaphoreType.REGULAR((len(PARTS),)),
        ],
        compiler_params=pltpu.CompilerParams(
            collective_id=0, has_side_effects=True, vmem_limit_bytes=VMEM_LIMIT
        ),
        name="sparse_attention",
    )(
        selections,
        index_weights.T,
        cache_latent.T,
        index_keys,
        cache_scales.T,
        queries,
        index_queries,
        value_up,
    )


def solution(mesh):
    return jax.shard_map(
        local,
        mesh=mesh,
        in_specs=(
            P("ctx", "head"),
            P("ctx", None),
            P("ctx", None),
            P("ctx", None),
            P("ctx", "head"),
            P("ctx", "head"),
            P("head", None, None),
            P("ctx", None),
        ),
        out_specs=(P("ctx", "head"), P("ctx", "head")),
        check_vma=False,
    )
```

```python
from functools import partial

import jax
import jax.numpy as jnp
from jax import lax
from jax.experimental import pallas as pl
from jax.experimental.pallas import tpu as pltpu
from jax.sharding import PartitionSpec as P

D_LAT = 512
D_ROPE = 64
NOPE_DIM = 128
D_HEAD = 128
IDX_DIM = 128
BLOCK = 64
SEL = 32
D_KEY = 576
LANES = 128
MESH = pl.DeviceIdType.MESH
BF16 = jnp.bfloat16
F32 = jnp.float32
KEY_ROWS = IDX_DIM // 4
ROPE_ROWS = D_ROPE // 4
PARTS = (KEY_ROWS + ROPE_ROWS, 32, 32, 32, 32)
STEP = 16
APART = 8
VMEM_LIMIT = 60 * 1024 * 1024


def loop(low, high, step, unroll=None):
    def body(i, carry):
        step(i)
        return carry

    lax.fori_loop(low, high, body, 0, unroll=unroll)


def lanes_at(i):
    return pl.ds(pl.multiple_of(i * LANES, LANES), LANES)


def kernel(
    n,
    heads,
    sel_ref,
    w_ref,
    lat_hbm,
    keys_hbm,
    scales_hbm,
    q_hbm,
    iq_hbm,
    up_hbm,
    out_ref,
    logits_ref,
    latq,
    ropeq,
    keyq,
    scl,
    q,
    iq,
    up,
    reqs,
    req_in,
    req_rows,
    req_smem,
    picks_v,
    picks,
    lows,
    sends,
    recvs,
    lat,
    tail,
    key,
    wcol,
    terms,
    terms_in,
    qs,
    qr,
    load_sem,
    req_send,
    req_recv,
    send_sem,
    recv_sem,
    xsend,
    xrecv,
    isend,
    irecv,
    ready,
):
    me = lax.axis_index("ctx")
    hx = lax.axis_index("head")
    group = D_LAT // 4
    wide = SEL * BLOCK
    tiles = latq.shape[1] // LANES
    parts = range(len(PARTS))
    starts = [sum(PARTS[1:p]) for p in parts]

    loads = [
        pltpu.make_async_copy(keys_hbm, keyq, load_sem.at[0]),
        pltpu.make_async_copy(
            lat_hbm.at[pl.ds(D_LAT + hx * ROPE_ROWS, ROPE_ROWS), :], ropeq, load_sem.at[1]
        ),
        pltpu.make_async_copy(scales_hbm, scl, load_sem.at[2]),
        pltpu.make_async_copy(lat_hbm.at[pl.ds(hx * group, group), :], latq, load_sem.at[3]),
    ]
    later = [
        pltpu.make_async_copy(iq_hbm, iq, load_sem.at[4]),
        pltpu.make_async_copy(q_hbm, q, load_sem.at[5]),
        pltpu.make_async_copy(up_hbm, up, load_sem.at[6]),
    ]
    for copy in loads:
        copy.start()
    req_in[...] = jnp.zeros_like(req_in)

    barrier = pltpu.get_barrier_semaphore()

    def greet(j):
        pl.semaphore_signal(
            barrier, inc=1, device_id=(lax.rem(me + j, n), hx), device_id_type=MESH
        )

    loop(1, n, greet)
    for j in range(1, heads):
        pl.semaphore_signal(
            barrier, inc=1, device_id=(me, lax.rem(hx + j, heads)), device_id_type=MESH
        )

    chosen = jnp.concatenate([sel_ref[0:1, :], sel_ref[1:2, :]], axis=1)
    count = 2 * SEL
    kblocks = 2 * tiles
    owners = chosen // kblocks
    inside = chosen - owners * kblocks
    square = (count, count)
    across = jnp.broadcast_to(chosen, square)
    diagonal = lax.broadcasted_iota(jnp.int32, square, 0) == lax.broadcasted_iota(
        jnp.int32, square, 1
    )
    down = jnp.sum(jnp.where(diagonal, across, 0), axis=1, keepdims=True)
    smaller = (down // kblocks == across // kblocks) & (down < across)
    rank = jnp.max(smaller.astype(jnp.int32), axis=0, keepdims=True)
    odd = lax.broadcasted_iota(jnp.int32, (1, count), 1) % 2
    here = (owners == me).astype(jnp.int32)
    picks_v[...] = jnp.zeros_like(picks_v)
    picks_v[0:1, 0:count] = jnp.where(here > 0, 0, owners)
    picks_v[1:2, 0:count] = jnp.where(here > 0, inside + odd - 2 * odd * (inside % 2), 0)
    picks_v[2:3, 0:count] = here
    picks_v[3:4, 0:count] = (rank != odd).astype(jnp.int32)
    for k in range(n // 8):
        owner = lax.broadcasted_iota(jnp.int32, (8, count), 0) + 8 * k
        mine = jnp.broadcast_to(owners, (8, count)) == owner
        blocks = jnp.broadcast_to(inside, (8, count))
        one = jnp.min(jnp.where(mine, blocks, kblocks - 1), axis=1, keepdims=True)
        two = jnp.max(jnp.where(mine, blocks, 0), axis=1, keepdims=True)
        two = two + 1 - 2 * (two % 2)
        lane = lax.broadcasted_iota(jnp.int32, (8, LANES), 1)
        reqs[k] = jnp.where(lane == 0, one, two)
    picks_copy = pltpu.make_async_copy(picks_v, picks, load_sem.at[7])
    picks_copy.start()

    rows_at = lax.broadcasted_iota(jnp.int32, (KEY_ROWS, IDX_DIM), 0) + hx * KEY_ROWS
    cols_at = lax.broadcasted_iota(jnp.int32, (KEY_ROWS, IDX_DIM), 1)
    take = (rows_at == cols_at).astype(BF16)
    group_at = lax.broadcasted_iota(jnp.int32, (4, LANES), 0)

    def keep(p, t, block):
        lows[p][2 * t] = block.astype(BF16)
        lows[p][2 * t + 1] = pltpu.roll(block, BLOCK, 1).astype(BF16)

    def dequantize_first(t):
        at = lanes_at(t)
        part = lax.dot_general(
            take, keyq[at, :], (((1,), (1,)), ((), ())), preferred_element_type=F32
        )
        part = part * scl[4:5, at]
        keep(0, t, jnp.concatenate([part, ropeq[:, at].astype(F32)], axis=0))

    def dequantize_rest(t):
        at = lanes_at(t)
        mine = jnp.sum(jnp.where(group_at == hx, scl[0:4, at], 0.0), axis=0, keepdims=True)
        part = latq[:, at].astype(F32) * mine
        for p in parts[1:]:
            keep(p, t, part[starts[p] : starts[p] + PARTS[p]])

    for copy in loads[:3]:
        copy.wait()
    loop(0, tiles, dequantize_first, 4)

    pl.semaphore_wait(barrier, n + heads - 2)

    def request(o, c):
        return pltpu.make_async_remote_copy(
            src_ref=reqs.at[o // 8],
            dst_ref=req_in.at[c],
            send_sem=req_send.at[o],
            recv_sem=req_recv.at[c],
            device_id=(o, hx),
            device_id_type=MESH,
        )

    loop(0, me, lambda o: request(o, me).start())

    loads[3].wait()
    loop(0, tiles, dequantize_rest, 4)
    loop(me + 1, n, lambda c: request(me, c).wait_recv())
    row_at = lax.broadcasted_iota(jnp.int32, (n, 8, LANES), 1)
    req_rows[...] = jnp.sum(jnp.where(row_at == lax.rem(me, 8), req_in[...], 0), axis=1)
    to_smem = pltpu.make_async_copy(req_rows, req_smem, load_sem.at[8])
    to_smem.start()
    to_smem.wait()

    def block_copy(p, c, o):
        return pltpu.make_async_remote_copy(
            src_ref=sends[p].at[c],
            dst_ref=recvs[p].at[o],
            send_sem=send_sem.at[p, c],
            recv_sem=recv_sem.at[p, o],
            device_id=(c, hx),
            device_id_type=MESH,
        )

    def pack(p, c):
        one = req_smem[c, 0]
        two = req_smem[c, 1]
        sends[p][c, :, 0:BLOCK] = lows[p][one][:, 0:BLOCK]
        sends[p][c, :, BLOCK:LANES] = lows[p][two][:, BLOCK:LANES]

    def pack_first(c):
        pack(0, c)
        block_copy(0, c, me).start()

    loop(me + 1, n, pack_first)
    for copy in later:
        copy.start()
    picks_copy.wait()

    def send(p):
        def step(c):
            pack(p, c)
            block_copy(p, c, me).start()

        if p > 1:
            watched = (n - 1 - me) // APART

            @pl.when(watched > 0)
            def _():
                pl.semaphore_wait(ready.at[p - 2], watched)

            loop(me + 1, n, lambda c: block_copy(p - 2, c, me).wait_send())
        loop(me + 1, n, step)

    def outs(p):
        if p == 0:
            return (
                (key, KEY_ROWS, 0, lambda part: part * KEY_ROWS),
                (tail, ROPE_ROWS, KEY_ROWS, lambda part: part * ROPE_ROWS),
            )
        return ((lat, PARTS[p], 0, lambda part: part * group + starts[p]),)

    right, left, across_x = lax.rem(hx + 1, heads), lax.rem(hx + 3, heads), lax.rem(hx + 2, heads)
    to_right, to_left, on_right, on_left = range(4)

    def share(p, i, out, way, part, peer):
        ref, rows, _, place = out
        at = pl.ds(pl.multiple_of(place(part), ROPE_ROWS), rows)
        piece = ref.at[way - 2, at, :] if way >= 2 else ref.at[:, at, :]
        return pltpu.make_async_remote_copy(
            src_ref=piece,
            dst_ref=piece,
            send_sem=xsend.at[p + len(PARTS) * i, way],
            recv_sem=xrecv.at[p + len(PARTS) * i, way],
            device_id=(me, peer),
            device_id_type=MESH,
        )

    peers = [right, left, across_x]

    def receive(p):
        loop(0, me, lambda o: block_copy(p, o, o).wait_recv())
        if p < len(PARTS) - 2:
            loop(
                1,
                me // APART + 1,
                lambda k: pl.semaphore_signal(
                    ready.at[p], inc=1, device_id=(me - APART * k, hx), device_id_type=MESH
                ),
            )
        low_lanes = lax.broadcasted_iota(jnp.int32, (PARTS[p], LANES), 1) < BLOCK

        def choose(m):
            def entry(e):
                far = recvs[p][picks[0, e]].astype(F32)
                far = jnp.where(picks[3, e] > 0, pltpu.roll(far, BLOCK, 1), far)
                near = lows[p][picks[1, e]].astype(F32)
                return jnp.where(picks[2, e] > 0, near, far)

            tile = jnp.where(low_lanes, entry(2 * m), entry(2 * m + 1)).astype(BF16)
            row = m // (SEL // 2)
            for ref, rows, first, place in outs(p):
                at = pl.ds(pl.multiple_of(place(hx), ROPE_ROWS), rows)
                ref[row, at, lanes_at(lax.rem(m, SEL // 2))] = tile[first : first + rows]

        loop(0, SEL, choose, 4)
        for i, out in enumerate(outs(p)):
            share(p, i, out, to_right, hx, right).start()
            share(p, i, out, to_left, hx, left).start()

    def forward(p):
        for i, out in enumerate(outs(p)):
            share(p, i, out, to_right, left, hx).wait_recv()
            share(p, i, out, on_right, left, right).start()
            share(p, i, out, to_left, right, hx).wait_recv()
            share(p, i, out, on_left, right, left).start()

    def shared(p):
        for i, out in enumerate(outs(p)):
            share(p, i, out, on_right, across_x, hx).wait_recv()
            share(p, i, out, on_left, across_x, hx).wait_recv()

    send(1)

    column = lax.broadcasted_iota(jnp.int32, (BLOCK, wide), 1)
    token = lax.broadcasted_iota(jnp.int32, (BLOCK, wide), 0)
    for r in range(2):
        own = me * kblocks + kblocks - 2 + r
        at = lax.broadcasted_iota(jnp.int32, (1, SEL), 1)
        place = jnp.sum(jnp.where(sel_ref[r : r + 1, :] == own, at, 0), axis=1, keepdims=True)
        hidden = (column // BLOCK == place) & (column % BLOCK > token)
        tail[r, D_ROPE:, :] = jnp.where(hidden, -1e30, 0.0).astype(BF16)
    wcol[...] = jnp.transpose(w_ref[...].astype(F32)) * IDX_DIM**-0.5

    receive(0)
    send(2)
    receive(1)
    forward(0)
    send(3)
    receive(2)
    forward(1)
    send(4)
    shared(0)

    later[0].wait()
    idx_here = wcol.shape[1]

    def index_rows(r):
        rows = pl.ds(pl.multiple_of(r * BLOCK, BLOCK), BLOCK)
        weights = wcol[rows, :]
        total = jnp.zeros((BLOCK, wide), F32)
        for g in range(idx_here):
            dots = jnp.dot(
                iq[rows, g * IDX_DIM : (g + 1) * IDX_DIM], key[r], preferred_element_type=F32
            )
            total += weights[:, g : g + 1] * jnp.maximum(dots, 0.0)
        total = jnp.where(tail[r, D_ROPE:, :].astype(F32) < 0.0, 0.0, total).astype(BF16)
        share_wide = wide // heads
        for h in range(heads):
            terms[h, rows, :] = total[:, h * share_wide : (h + 1) * share_wide]

    loop(0, 2, index_rows)

    def term(part, peer):
        return pltpu.make_async_remote_copy(
            src_ref=terms.at[peer],
            dst_ref=terms_in.at[part],
            send_sem=isend.at[peer],
            recv_sem=irecv.at[part],
            device_id=(me, peer),
            device_id_type=MESH,
        )

    for peer in peers:
        term(hx, peer).start()

    later[1].wait()
    same = (
        lax.broadcasted_iota(jnp.int32, (BLOCK, BLOCK), 0)
        == lax.broadcasted_iota(jnp.int32, (BLOCK, BLOCK), 1)
    ).astype(BF16)
    groups = up.shape[0] // STEP

    def arrange(i):
        r, g = i // groups, lax.rem(i, groups)
        part = q[
            pl.ds(pl.multiple_of(r * BLOCK, BLOCK), BLOCK),
            pl.ds(pl.multiple_of(g * STEP * D_KEY, LANES), STEP * D_KEY),
        ]
        for h in range(STEP):
            rows = slice(h * BLOCK, (h + 1) * BLOCK)
            qs[i, rows, :] = part[:, h * D_KEY : h * D_KEY + D_LAT]
            qr[i, rows, :D_ROPE] = part[:, h * D_KEY + D_LAT : (h + 1) * D_KEY]
            qr[i, rows, D_ROPE:] = same

    loop(0, 2 * groups, arrange)
    receive(3)
    forward(2)
    for peer in peers:
        term(peer, hx).wait_recv()
    logits = terms[hx].astype(F32)
    for peer in peers:
        logits += terms_in[peer].astype(F32)
    logits_ref[...] = logits

    receive(4)
    forward(3)
    forward(4)
    for p in parts[3:]:
        loop(me + 1, n, lambda c, p=p: block_copy(p, c, me).wait_send())

    later[2].wait()
    for p in parts[1:]:
        shared(p)

    def attend(i):
        r, g = i // groups, lax.rem(i, groups)
        scores = jnp.dot(qs[i], lat[r], preferred_element_type=F32)
        scores += jnp.dot(qr[i], tail[r], preferred_element_type=F32)
        top = jnp.max(scores, axis=1, keepdims=True)
        scale = (NOPE_DIM + D_ROPE) ** -0.5 * 1.4426950408889634
        weights = jnp.exp2((scores - top) * scale)
        total = jnp.sum(weights, axis=1, keepdims=True)
        attended = lax.dot_general(
            weights.astype(BF16), lat[r], (((1,), (1,)), ((), ())), preferred_element_type=F32
        )
        attended = (attended / total).astype(BF16)
        rows = pl.ds(pl.multiple_of(r * BLOCK, BLOCK), BLOCK)
        for h in range(STEP):
            out = jnp.dot(
                attended[h * BLOCK : (h + 1) * BLOCK], up[g * STEP + h], preferred_element_type=F32
            )
            out_ref[rows, lanes_at(g * STEP + h)] = out.astype(BF16)

    loop(0, 2 * groups, attend)

    for p in parts:
        for i, out in enumerate(outs(p)):
            share(p, i, out, to_right, hx, right).wait_send()
            share(p, i, out, to_left, hx, left).wait_send()
            share(p, i, out, on_right, left, right).wait_send()
            share(p, i, out, on_left, right, left).wait_send()
    for peer in peers:
        term(hx, peer).wait_send()
    loop(0, me, lambda o: request(o, me).wait_send())


def local(
    queries,
    cache_latent,
    cache_scales,
    index_keys,
    index_queries,
    index_weights,
    value_up,
    selections,
):
    n = lax.axis_size("ctx")
    heads = lax.axis_size("head")
    tokens = index_keys.shape[0]
    qtokens = queries.shape[0]
    kblocks = tokens // BLOCK
    heads_here = value_up.shape[0]
    idx_here = index_weights.shape[1]
    wide = SEL * BLOCK
    any_spec = pl.BlockSpec(memory_space=pl.ANY)
    vmem_spec = pl.BlockSpec(memory_space=pltpu.VMEM)
    dma = pltpu.SemaphoreType.DMA
    vmem = pltpu.VMEM
    steps = 2 * heads_here // STEP
    return pl.pallas_call(
        partial(kernel, n, heads),
        out_shape=(
            jax.ShapeDtypeStruct((qtokens, heads_here * D_HEAD), BF16),
            jax.ShapeDtypeStruct((qtokens, wide // heads), F32),
        ),
        in_specs=[vmem_spec] * 2 + [any_spec] * 6,
        out_specs=(vmem_spec,) * 2,
        scratch_shapes=[
            vmem((D_LAT // 4, tokens), BF16),
            vmem((ROPE_ROWS, tokens), BF16),
            vmem((tokens, IDX_DIM), BF16),
            vmem((5, tokens), F32),
            vmem(queries.shape, BF16),
            vmem(index_queries.shape, BF16),
            vmem(value_up.shape, BF16),
            vmem((n // 8, 8, LANES), jnp.int32),
            vmem((n, 8, LANES), jnp.int32),
            vmem((n, LANES), jnp.int32),
            pltpu.SMEM((n, LANES), jnp.int32),
            vmem((8, LANES), jnp.int32),
            pltpu.SMEM((8, LANES), jnp.int32),
            [vmem((kblocks, rows, LANES), BF16) for rows in PARTS],
            [vmem((n, rows, LANES), BF16) for rows in PARTS],
            [vmem((n, rows, LANES), BF16) for rows in PARTS],
            vmem((2, D_LAT, wide), BF16),
            vmem((2, D_ROPE + BLOCK, wide), BF16),
            vmem((2, IDX_DIM, wide), BF16),
            vmem((qtokens, idx_here), F32),
            vmem((heads, qtokens, wide // heads), BF16),
            vmem((heads, qtokens, wide // heads), BF16),
            vmem((steps, STEP * BLOCK, D_LAT), BF16),
            vmem((steps, STEP * BLOCK, 2 * D_ROPE), BF16),
            dma((9,)),
            dma((n,)),
            dma((n,)),
            dma((len(PARTS), n)),
            dma((len(PARTS), n)),
            dma((len(PARTS) + 1, heads)),
            dma((len(PARTS) + 1, heads)),
            dma((heads,)),
            dma((heads,)),
            pltpu.SemaphoreType.REGULAR((len(PARTS),)),
        ],
        compiler_params=pltpu.CompilerParams(
            collective_id=0, has_side_effects=True, vmem_limit_bytes=VMEM_LIMIT
        ),
        name="sparse_attention",
    )(
        selections,
        index_weights.T,
        cache_latent.T,
        index_keys,
        cache_scales.T,
        queries,
        index_queries,
        value_up,
    )


def solution(mesh):
    return jax.shard_map(
        local,
        mesh=mesh,
        in_specs=(
            P("ctx", "head"),
            P("ctx", None),
            P("ctx", None),
            P("ctx", None),
            P("ctx", "head"),
            P("ctx", "head"),
            P("head", None, None),
            P("ctx", None),
        ),
        out_specs=(P("ctx", "head"), P("ctx", "head")),
        check_vma=False,
    )
```

```python
from functools import partial

import jax
import jax.numpy as jnp
from jax import lax
from jax.experimental import pallas as pl
from jax.experimental.pallas import tpu as pltpu
from jax.sharding import PartitionSpec as P

D_LAT = 512
D_ROPE = 64
NOPE_DIM = 128
D_HEAD = 128
IDX_DIM = 128
BLOCK = 64
SEL = 32
D_KEY = 576
LANES = 128
MESH = pl.DeviceIdType.MESH
BF16 = jnp.bfloat16
F32 = jnp.float32
KEY_ROWS = IDX_DIM // 4
ROPE_ROWS = D_ROPE // 4
PARTS = (KEY_ROWS + ROPE_ROWS, 32, 32, 32, 32)
STEP = 16
APART = 8
VMEM_LIMIT = 60 * 1024 * 1024


def loop(low, high, step, unroll=None):
    def body(i, carry):
        step(i)
        return carry

    lax.fori_loop(low, high, body, 0, unroll=unroll)


def lanes_at(i):
    return pl.ds(pl.multiple_of(i * LANES, LANES), LANES)


def kernel(
    n,
    heads,
    sel_ref,
    w_ref,
    lat_hbm,
    keys_hbm,
    scales_hbm,
    q_hbm,
    iq_hbm,
    up_hbm,
    out_ref,
    logits_ref,
    latq,
    ropeq,
    keyq,
    scl,
    q,
    iq,
    up,
    reqs,
    req_in,
    req_rows,
    req_smem,
    picks_v,
    picks,
    lows,
    sends,
    recvs,
    lat,
    tail,
    key,
    wcol,
    terms,
    terms_in,
    qs,
    qr,
    load_sem,
    req_send,
    req_recv,
    send_sem,
    recv_sem,
    xsend,
    xrecv,
    isend,
    irecv,
    ready,
):
    me = lax.axis_index("ctx")
    hx = lax.axis_index("head")
    group = D_LAT // 4
    wide = SEL * BLOCK
    tiles = latq.shape[1] // LANES
    parts = range(len(PARTS))
    starts = [sum(PARTS[1:p]) for p in parts]

    loads = [
        pltpu.make_async_copy(keys_hbm, keyq, load_sem.at[0]),
        pltpu.make_async_copy(
            lat_hbm.at[pl.ds(D_LAT + hx * ROPE_ROWS, ROPE_ROWS), :], ropeq, load_sem.at[1]
        ),
        pltpu.make_async_copy(scales_hbm, scl, load_sem.at[2]),
        pltpu.make_async_copy(lat_hbm.at[pl.ds(hx * group, group), :], latq, load_sem.at[3]),
    ]
    later = [
        pltpu.make_async_copy(iq_hbm, iq, load_sem.at[4]),
        pltpu.make_async_copy(q_hbm, q, load_sem.at[5]),
        pltpu.make_async_copy(up_hbm, up, load_sem.at[6]),
    ]
    for copy in loads:
        copy.start()
    req_in[...] = jnp.zeros_like(req_in)

    barrier = pltpu.get_barrier_semaphore()

    def greet(j):
        pl.semaphore_signal(
            barrier, inc=1, device_id=(lax.rem(me + j, n), hx), device_id_type=MESH
        )

    loop(1, n, greet)
    for j in range(1, heads):
        pl.semaphore_signal(
            barrier, inc=1, device_id=(me, lax.rem(hx + j, heads)), device_id_type=MESH
        )

    chosen = jnp.concatenate([sel_ref[0:1, :], sel_ref[1:2, :]], axis=1)
    count = 2 * SEL
    kblocks = 2 * tiles
    owners = chosen // kblocks
    inside = chosen - owners * kblocks
    square = (count, count)
    across = jnp.broadcast_to(chosen, square)
    diagonal = lax.broadcasted_iota(jnp.int32, square, 0) == lax.broadcasted_iota(
        jnp.int32, square, 1
    )
    down = jnp.sum(jnp.where(diagonal, across, 0), axis=1, keepdims=True)
    smaller = (down // kblocks == across // kblocks) & (down < across)
    rank = jnp.max(smaller.astype(jnp.int32), axis=0, keepdims=True)
    odd = lax.broadcasted_iota(jnp.int32, (1, count), 1) % 2
    here = (owners == me).astype(jnp.int32)
    picks_v[...] = jnp.zeros_like(picks_v)
    picks_v[0:1, 0:count] = jnp.where(here > 0, 0, owners)
    picks_v[1:2, 0:count] = jnp.where(here > 0, inside + odd - 2 * odd * (inside % 2), 0)
    picks_v[2:3, 0:count] = here
    picks_v[3:4, 0:count] = (rank != odd).astype(jnp.int32)
    for k in range(n // 8):
        owner = lax.broadcasted_iota(jnp.int32, (8, count), 0) + 8 * k
        mine = jnp.broadcast_to(owners, (8, count)) == owner
        blocks = jnp.broadcast_to(inside, (8, count))
        one = jnp.min(jnp.where(mine, blocks, kblocks - 1), axis=1, keepdims=True)
        two = jnp.max(jnp.where(mine, blocks, 0), axis=1, keepdims=True)
        two = two + 1 - 2 * (two % 2)
        lane = lax.broadcasted_iota(jnp.int32, (8, LANES), 1)
        reqs[k] = jnp.where(lane == 0, one, two)
    picks_copy = pltpu.make_async_copy(picks_v, picks, load_sem.at[7])
    picks_copy.start()

    rows_at = lax.broadcasted_iota(jnp.int32, (KEY_ROWS, IDX_DIM), 0) + hx * KEY_ROWS
    cols_at = lax.broadcasted_iota(jnp.int32, (KEY_ROWS, IDX_DIM), 1)
    take = (rows_at == cols_at).astype(BF16)
    group_at = lax.broadcasted_iota(jnp.int32, (4, LANES), 0)

    def keep(p, t, block):
        lows[p][2 * t] = block.astype(BF16)
        lows[p][2 * t + 1] = pltpu.roll(block, BLOCK, 1).astype(BF16)

    def dequantize_first(t):
        at = lanes_at(t)
        part = lax.dot_general(
            take, keyq[at, :], (((1,), (1,)), ((), ())), preferred_element_type=F32
        )
        part = part * scl[4:5, at]
        keep(0, t, jnp.concatenate([part, ropeq[:, at].astype(F32)], axis=0))

    def dequantize_rest(t):
        at = lanes_at(t)
        mine = jnp.sum(jnp.where(group_at == hx, scl[0:4, at], 0.0), axis=0, keepdims=True)
        part = latq[:, at].astype(F32) * mine
        for p in parts[1:]:
            keep(p, t, part[starts[p] : starts[p] + PARTS[p]])

    for copy in loads[:3]:
        copy.wait()
    loop(0, tiles, dequantize_first, 4)

    pl.semaphore_wait(barrier, n + heads - 2)

    def request(o, c):
        return pltpu.make_async_remote_copy(
            src_ref=reqs.at[o // 8],
            dst_ref=req_in.at[c],
            send_sem=req_send.at[o],
            recv_sem=req_recv.at[c],
            device_id=(o, hx),
            device_id_type=MESH,
        )

    loop(0, me, lambda o: request(o, me).start())

    loads[3].wait()
    loop(0, tiles, dequantize_rest, 4)
    loop(me + 1, n, lambda c: request(me, c).wait_recv())
    row_at = lax.broadcasted_iota(jnp.int32, (n, 8, LANES), 1)
    req_rows[...] = jnp.sum(jnp.where(row_at == lax.rem(me, 8), req_in[...], 0), axis=1)
    to_smem = pltpu.make_async_copy(req_rows, req_smem, load_sem.at[8])
    to_smem.start()
    to_smem.wait()

    def block_copy(p, c, o):
        return pltpu.make_async_remote_copy(
            src_ref=sends[p].at[c],
            dst_ref=recvs[p].at[o],
            send_sem=send_sem.at[p, c],
            recv_sem=recv_sem.at[p, o],
            device_id=(c, hx),
            device_id_type=MESH,
        )

    def pack(p, c):
        one = req_smem[c, 0]
        two = req_smem[c, 1]
        sends[p][c, :, 0:BLOCK] = lows[p][one][:, 0:BLOCK]
        sends[p][c, :, BLOCK:LANES] = lows[p][two][:, BLOCK:LANES]

    def pack_first(c):
        pack(0, c)
        block_copy(0, c, me).start()

    halfway = me + 1 + (n - 1 - me) // 2
    loop(halfway, n, pack_first)
    loop(me + 1, halfway, pack_first)
    for copy in later:
        copy.start()
    picks_copy.wait()

    def send(p):
        def step(c):
            pack(p, c)
            block_copy(p, c, me).start()

        if p > 1:
            watched = (n - 1 - me) // APART

            @pl.when(watched > 0)
            def _():
                pl.semaphore_wait(ready.at[p - 2], watched)

            loop(me + 1, n, lambda c: block_copy(p - 2, c, me).wait_send())
        loop(halfway, n, step)
        loop(me + 1, halfway, step)

    def outs(p):
        if p == 0:
            return (
                (key, KEY_ROWS, 0, lambda part: part * KEY_ROWS),
                (tail, ROPE_ROWS, KEY_ROWS, lambda part: part * ROPE_ROWS),
            )
        return ((lat, PARTS[p], 0, lambda part: part * group + starts[p]),)

    right, left, across_x = lax.rem(hx + 1, heads), lax.rem(hx + 3, heads), lax.rem(hx + 2, heads)
    to_right, to_left, on_right, on_left = range(4)

    def share(p, i, out, way, part, peer):
        ref, rows, _, place = out
        at = pl.ds(pl.multiple_of(place(part), ROPE_ROWS), rows)
        piece = ref.at[way - 2, at, :] if way >= 2 else ref.at[:, at, :]
        return pltpu.make_async_remote_copy(
            src_ref=piece,
            dst_ref=piece,
            send_sem=xsend.at[p + len(PARTS) * i, way],
            recv_sem=xrecv.at[p + len(PARTS) * i, way],
            device_id=(me, peer),
            device_id_type=MESH,
        )

    peers = [right, left, across_x]

    def receive(p):
        loop(0, me, lambda o: block_copy(p, o, o).wait_recv())
        if p < len(PARTS) - 2:
            loop(
                1,
                me // APART + 1,
                lambda k: pl.semaphore_signal(
                    ready.at[p], inc=1, device_id=(me - APART * k, hx), device_id_type=MESH
                ),
            )
        low_lanes = lax.broadcasted_iota(jnp.int32, (PARTS[p], LANES), 1) < BLOCK

        def choose(m):
            def entry(e):
                far = recvs[p][picks[0, e]].astype(F32)
                far = jnp.where(picks[3, e] > 0, pltpu.roll(far, BLOCK, 1), far)
                near = lows[p][picks[1, e]].astype(F32)
                return jnp.where(picks[2, e] > 0, near, far)

            tile = jnp.where(low_lanes, entry(2 * m), entry(2 * m + 1)).astype(BF16)
            row = m // (SEL // 2)
            for ref, rows, first, place in outs(p):
                at = pl.ds(pl.multiple_of(place(hx), ROPE_ROWS), rows)
                ref[row, at, lanes_at(lax.rem(m, SEL // 2))] = tile[first : first + rows]

        loop(0, SEL, choose, 4)
        for i, out in enumerate(outs(p)):
            share(p, i, out, to_right, hx, right).start()
            share(p, i, out, to_left, hx, left).start()

    def forward(p):
        for i, out in enumerate(outs(p)):
            share(p, i, out, to_right, left, hx).wait_recv()
            share(p, i, out, on_right, left, right).start()
            share(p, i, out, to_left, right, hx).wait_recv()
            share(p, i, out, on_left, right, left).start()

    def shared(p):
        for i, out in enumerate(outs(p)):
            share(p, i, out, on_right, across_x, hx).wait_recv()
            share(p, i, out, on_left, across_x, hx).wait_recv()

    send(1)

    column = lax.broadcasted_iota(jnp.int32, (BLOCK, wide), 1)
    token = lax.broadcasted_iota(jnp.int32, (BLOCK, wide), 0)
    for r in range(2):
        own = me * kblocks + kblocks - 2 + r
        at = lax.broadcasted_iota(jnp.int32, (1, SEL), 1)
        place = jnp.sum(jnp.where(sel_ref[r : r + 1, :] == own, at, 0), axis=1, keepdims=True)
        hidden = (column // BLOCK == place) & (column % BLOCK > token)
        tail[r, D_ROPE:, :] = jnp.where(hidden, -1e30, 0.0).astype(BF16)
    wcol[...] = jnp.transpose(w_ref[...].astype(F32)) * IDX_DIM**-0.5

    receive(0)
    send(2)
    receive(1)
    forward(0)
    send(3)
    receive(2)
    forward(1)
    send(4)
    shared(0)

    later[0].wait()
    idx_here = wcol.shape[1]

    def index_rows(r):
        rows = pl.ds(pl.multiple_of(r * BLOCK, BLOCK), BLOCK)
        weights = wcol[rows, :]
        total = jnp.zeros((BLOCK, wide), F32)
        for g in range(idx_here):
            dots = jnp.dot(
                iq[rows, g * IDX_DIM : (g + 1) * IDX_DIM], key[r], preferred_element_type=F32
            )
            total += weights[:, g : g + 1] * jnp.maximum(dots, 0.0)
        total = jnp.where(tail[r, D_ROPE:, :].astype(F32) < 0.0, 0.0, total).astype(BF16)
        share_wide = wide // heads
        for h in range(heads):
            terms[h, rows, :] = total[:, h * share_wide : (h + 1) * share_wide]

    loop(0, 2, index_rows)

    def term(part, peer):
        return pltpu.make_async_remote_copy(
            src_ref=terms.at[peer],
            dst_ref=terms_in.at[part],
            send_sem=isend.at[peer],
            recv_sem=irecv.at[part],
            device_id=(me, peer),
            device_id_type=MESH,
        )

    for peer in peers:
        term(hx, peer).start()

    later[1].wait()
    same = (
        lax.broadcasted_iota(jnp.int32, (BLOCK, BLOCK), 0)
        == lax.broadcasted_iota(jnp.int32, (BLOCK, BLOCK), 1)
    ).astype(BF16)
    groups = up.shape[0] // STEP

    def arrange(i):
        r, g = i // groups, lax.rem(i, groups)
        part = q[
            pl.ds(pl.multiple_of(r * BLOCK, BLOCK), BLOCK),
            pl.ds(pl.multiple_of(g * STEP * D_KEY, LANES), STEP * D_KEY),
        ]
        for h in range(STEP):
            rows = slice(h * BLOCK, (h + 1) * BLOCK)
            qs[i, rows, :] = part[:, h * D_KEY : h * D_KEY + D_LAT]
            qr[i, rows, :D_ROPE] = part[:, h * D_KEY + D_LAT : (h + 1) * D_KEY]
            qr[i, rows, D_ROPE:] = same

    loop(0, 2 * groups, arrange)
    receive(3)
    forward(2)
    for peer in peers:
        term(peer, hx).wait_recv()
    logits = terms[hx].astype(F32)
    for peer in peers:
        logits += terms_in[peer].astype(F32)
    logits_ref[...] = logits

    receive(4)
    forward(3)
    forward(4)
    for p in parts[3:]:
        loop(me + 1, n, lambda c, p=p: block_copy(p, c, me).wait_send())

    later[2].wait()
    for p in parts[1:]:
        shared(p)

    def attend(i):
        r, g = i // groups, lax.rem(i, groups)
        scores = jnp.dot(qs[i], lat[r], preferred_element_type=F32)
        scores += jnp.dot(qr[i], tail[r], preferred_element_type=F32)
        top = jnp.max(scores, axis=1, keepdims=True)
        scale = (NOPE_DIM + D_ROPE) ** -0.5 * 1.4426950408889634
        weights = jnp.exp2((scores - top) * scale)
        total = jnp.sum(weights, axis=1, keepdims=True)
        attended = lax.dot_general(
            weights.astype(BF16), lat[r], (((1,), (1,)), ((), ())), preferred_element_type=F32
        )
        attended = (attended / total).astype(BF16)
        rows = pl.ds(pl.multiple_of(r * BLOCK, BLOCK), BLOCK)
        for h in range(STEP):
            out = jnp.dot(
                attended[h * BLOCK : (h + 1) * BLOCK], up[g * STEP + h], preferred_element_type=F32
            )
            out_ref[rows, lanes_at(g * STEP + h)] = out.astype(BF16)

    loop(0, 2 * groups, attend)

    for p in parts:
        for i, out in enumerate(outs(p)):
            share(p, i, out, to_right, hx, right).wait_send()
            share(p, i, out, to_left, hx, left).wait_send()
            share(p, i, out, on_right, left, right).wait_send()
            share(p, i, out, on_left, right, left).wait_send()
    for peer in peers:
        term(hx, peer).wait_send()
    loop(0, me, lambda o: request(o, me).wait_send())


def local(
    queries,
    cache_latent,
    cache_scales,
    index_keys,
    index_queries,
    index_weights,
    value_up,
    selections,
):
    n = lax.axis_size("ctx")
    heads = lax.axis_size("head")
    tokens = index_keys.shape[0]
    qtokens = queries.shape[0]
    kblocks = tokens // BLOCK
    heads_here = value_up.shape[0]
    idx_here = index_weights.shape[1]
    wide = SEL * BLOCK
    any_spec = pl.BlockSpec(memory_space=pl.ANY)
    vmem_spec = pl.BlockSpec(memory_space=pltpu.VMEM)
    dma = pltpu.SemaphoreType.DMA
    vmem = pltpu.VMEM
    steps = 2 * heads_here // STEP
    return pl.pallas_call(
        partial(kernel, n, heads),
        out_shape=(
            jax.ShapeDtypeStruct((qtokens, heads_here * D_HEAD), BF16),
            jax.ShapeDtypeStruct((qtokens, wide // heads), F32),
        ),
        in_specs=[vmem_spec] * 2 + [any_spec] * 6,
        out_specs=(vmem_spec,) * 2,
        scratch_shapes=[
            vmem((D_LAT // 4, tokens), BF16),
            vmem((ROPE_ROWS, tokens), BF16),
            vmem((tokens, IDX_DIM), BF16),
            vmem((5, tokens), F32),
            vmem(queries.shape, BF16),
            vmem(index_queries.shape, BF16),
            vmem(value_up.shape, BF16),
            vmem((n // 8, 8, LANES), jnp.int32),
            vmem((n, 8, LANES), jnp.int32),
            vmem((n, LANES), jnp.int32),
            pltpu.SMEM((n, LANES), jnp.int32),
            vmem((8, LANES), jnp.int32),
            pltpu.SMEM((8, LANES), jnp.int32),
            [vmem((kblocks, rows, LANES), BF16) for rows in PARTS],
            [vmem((n, rows, LANES), BF16) for rows in PARTS],
            [vmem((n, rows, LANES), BF16) for rows in PARTS],
            vmem((2, D_LAT, wide), BF16),
            vmem((2, D_ROPE + BLOCK, wide), BF16),
            vmem((2, IDX_DIM, wide), BF16),
            vmem((qtokens, idx_here), F32),
            vmem((heads, qtokens, wide // heads), BF16),
            vmem((heads, qtokens, wide // heads), BF16),
            vmem((steps, STEP * BLOCK, D_LAT), BF16),
            vmem((steps, STEP * BLOCK, 2 * D_ROPE), BF16),
            dma((9,)),
            dma((n,)),
            dma((n,)),
            dma((len(PARTS), n)),
            dma((len(PARTS), n)),
            dma((len(PARTS) + 1, heads)),
            dma((len(PARTS) + 1, heads)),
            dma((heads,)),
            dma((heads,)),
            pltpu.SemaphoreType.REGULAR((len(PARTS),)),
        ],
        compiler_params=pltpu.CompilerParams(
            collective_id=0, has_side_effects=True, vmem_limit_bytes=VMEM_LIMIT
        ),
        name="sparse_attention",
    )(
        selections,
        index_weights.T,
        cache_latent.T,
        index_keys,
        cache_scales.T,
        queries,
        index_queries,
        value_up,
    )


def solution(mesh):
    return jax.shard_map(
        local,
        mesh=mesh,
        in_specs=(
            P("ctx", "head"),
            P("ctx", None),
            P("ctx", None),
            P("ctx", None),
            P("ctx", "head"),
            P("ctx", "head"),
            P("head", None, None),
            P("ctx", None),
        ),
        out_specs=(P("ctx", "head"), P("ctx", "head")),
        check_vma=False,
    )
```
